256 devices in a mesh: grp: 8 (over x, core), row: 8 (over y, z_lo), col: 4 (over z_hi).
Axes of the slice: x: 4, y: 4, z: 8 (z_hi: 4, z_lo: 2; z = z_hi * 2 + z_lo), core: 2. Of those that a mesh axis runs over, the one named last changes fastest.
Arguments:
- root_inverse: float32 [4096, 4096], P('row', ('grp', 'col')), as said below
- panel_middle: float32 [3072, 4096], P('row', ('grp', 'col')), may hold values from -0.3125 to 0.3125
- pivot_middle: float32 [2048, 4096], P('row', ('grp', 'col')), as said below
- panel_lower: float32 [1024, 4096], P('row', ('grp', 'col')), may hold values from -0.1875 to 0.1875
- pivot_lower: float32 [1024, 4096], P('row', ('grp', 'col')), as said below
- tiles_middle: int32 [2, 24], replicated, may hold values from 0 to 31, as said below
- tiles_lower: int32 [4, 8], replicated, may hold values from 0 to 15, as said below
Outputs:
- border_middle: float32 [3072, 4096], P('row', ('grp', 'col'))
- inverse_middle: float32 [2048, 4096], P('row', ('grp', 'col'))
- border_lower: float32 [1024, 4096], P('row', ('grp', 'col'))
- inverse_lower: float32 [1024, 4096], P('row', ('grp', 'col'))
The draws below stay inside these ranges and needn't reach their ends.
Inputs may be any that keep to these rules, and one draw needn't show every extreme that they name: `tiles_middle`: each row lists distinct tiles of the root separator, in no particular order; row 0 holds tile 0 and row 1 holds tile 32 - 1. `tiles_lower`: row f lists distinct tiles of the separator of middle front f // 2, in no particular order; even rows hold tile 0, odd rows hold tile 16 - 1. `root_inverse`: exactly symmetric. `pivot_middle`: each front's block is exactly symmetric. `pivot_lower`: each front's block is exactly symmetric.
All inputs are finite; a program needn't handle non-finite values.
Results may differ from the reference program's by a relative error of at most 0.0001.
Values sent between devices are 32-bit elements; how exact they have to be, the bound alone decides.
No kernel may reach another device: no remote copies, remote signals or barrier semaphores. Data moves between devices by JAX's collectives and lax.ppermute only.
A program may use at most 128 MiB of HBM per device.

```python
import math
import jax
import jax.numpy as jnp
from jax import lax

TILE = 128
S0 = 4096
U1 = 3072
S1 = 2048
U2 = 1024
S2 = 1024


def symmetric_blocks(key, count, size, spread):
    first, second, third = jax.random.split(key, 3)
    base = jax.random.normal(first, (count, size, size), jnp.float32)
    mixed = (base + jnp.swapaxes(base, 1, 2)) * (0.4 / math.sqrt(2.0 * size))
    diagonal = jax.random.uniform(second, (count, size), jnp.float32, 1.0, 2.0)
    scales = jnp.exp(jax.random.uniform(third, (count, size), jnp.float32, -spread, spread))
    identity = jnp.arange(size)[:, None] == jnp.arange(size)[None, :]
    matrix = jnp.where(identity[None], diagonal[:, :, None], mixed)
    return matrix * scales[:, :, None] * scales[:, None, :]


def listed_tiles(key, count, pool, chosen):
    listed = []
    middle = chosen // 2
    for front_index in range(count):
        order = jax.random.permutation(jax.random.fold_in(key, front_index), pool - 2).astype(jnp.int32) + 1
        ending = 0 if front_index % 2 == 0 else pool - 1
        others = order[:chosen - 1]
        picked = jnp.concatenate([others[:middle], jnp.array([ending], jnp.int32), others[middle:]])
        listed.append(picked)
    return jnp.stack(listed).astype(jnp.int32)


def draw_root_inverse(key, part):
    key = jax.random.fold_in(key, 3)
    spread = 0.0
    return symmetric_blocks(key, 1, S0, spread)[0]


def draw_pivot_middle(key, part):
    key = jax.random.fold_in(key, 5)
    spread = 0.0
    blocks = symmetric_blocks(key, 2, S1, spread)
    return jnp.transpose(blocks, (1, 0, 2)).reshape(S1, 2 * S1)


def draw_pivot_lower(key, part):
    key = jax.random.fold_in(key, 7)
    spread = 0.0
    blocks = symmetric_blocks(key, 4, S2, spread)
    return jnp.transpose(blocks, (1, 0, 2)).reshape(S2, 4 * S2)


def draw_tiles_middle(key, part):
    key = jax.random.fold_in(key, 11)
    return listed_tiles(key, 2, S0 // TILE, U1 // TILE)


def draw_tiles_lower(key, part):
    key = jax.random.fold_in(key, 13)
    return listed_tiles(key, 4, S1 // TILE, U2 // TILE)


def block_levels(own_key, extent, cuts, least, top_value):
    def one(axis_at, shards_of):
        draws = jax.random.uniform(jax.random.fold_in(jax.random.fold_in(own_key, 6), axis_at), (shards_of,), jnp.float32, least / len(cuts), top_value / len(cuts))
        return jnp.repeat(jnp.exp(draws), extent[axis_at] // shards_of).reshape((-1,) + (1,) * (len(extent) - axis_at - 1))

    level = one(*cuts[0])
    for cut in cuts[1:]:
        level = level * one(*cut)
    return level


def bell_draw(stream_key, extent, deviation, most, cuts=(), held_as=jnp.bfloat16):
    entries = jax.random.normal(stream_key, extent, jnp.float32) * deviation
    if len(cuts) > 0:
        entries = block_levels(stream_key, extent, cuts, -0.22, 0.18) * entries
    return jnp.clip(entries, min=-most, max=most).astype(held_as)


def setup_inputs(seed: int = 0) -> dict:
    arg_keys = jax.random.split(jax.random.key(seed), 8)
    return {
        "root_inverse": draw_root_inverse(jax.random.fold_in(arg_keys[7], 71), 0),
        "panel_middle": bell_draw(arg_keys[1], (U1, 2 * S1), (U1 // 9) ** -0.5, 0.3125, ((0, 8), (1, 32)), jnp.float32),
        "pivot_middle": draw_pivot_middle(jax.random.fold_in(arg_keys[7], 71), 0),
        "panel_lower": bell_draw(arg_keys[3], (U2, 4 * S2), U2 ** -0.5, 0.1875, ((0, 8), (1, 32)), jnp.float32),
        "pivot_lower": draw_pivot_lower(jax.random.fold_in(arg_keys[7], 71), 0),
        "tiles_middle": draw_tiles_middle(jax.random.fold_in(arg_keys[7], 71), 0),
        "tiles_lower": draw_tiles_lower(jax.random.fold_in(arg_keys[7], 71), 0),
    }


def spread_rows(tiles):
    offsets = jnp.arange(TILE, dtype=jnp.int32)
    return (tiles[:, None].astype(jnp.int32) * TILE + offsets[None, :]).reshape(-1)


def front_level(ancestors, tiles, panel, pivot, count, width):
    borders = []
    inverses = []
    for front_index in range(count):
        source = ancestors[front_index * len(ancestors) // count]
        rows = spread_rows(tiles[front_index])
        block = jnp.take(jnp.take(source, rows, axis=0), rows, axis=1)
        piece = panel[:, front_index * width:(front_index + 1) * width]
        border = -jnp.dot(block, piece, precision=lax.Precision.HIGHEST, preferred_element_type=jnp.float32)
        inverse = pivot[:, front_index * width:(front_index + 1) * width] - jnp.dot(
            piece.T, border, precision=lax.Precision.HIGHEST, preferred_element_type=jnp.float32)
        borders.append(border)
        inverses.append(inverse)
    return jnp.concatenate(borders, axis=1), jnp.concatenate(inverses, axis=1), inverses


def reference(root_inverse, panel_middle, pivot_middle, panel_lower, pivot_lower, tiles_middle, tiles_lower):
    border_middle, inverse_middle, blocks = front_level([root_inverse], tiles_middle, panel_middle, pivot_middle, 2, S1)
    border_lower, inverse_lower, unused_blocks = front_level(blocks, tiles_lower, panel_lower, pivot_lower, 4, S2)
    return border_middle, inverse_middle, border_lower, inverse_lower
```

```python
import functools

import jax
import jax.numpy as jnp
from jax import lax
from jax.experimental import pallas as pl
from jax.experimental.pallas import tpu as pltpu
from jax.sharding import PartitionSpec as P

TILE = 128
AXES = ("grp", "row", "col")
VMEM_LIMIT = 40 * 1024 * 1024


def shifted(value, axis, step):
    size = lax.axis_size(axis)
    return lax.ppermute(value, axis, [(i, (i - step) % size) for i in range(size)])


def crossed(value, axis, mask):
    size = lax.axis_size(axis)
    return lax.ppermute(value, axis, [(i, i ^ mask) for i in range(size)])


def ring(value, axis, unit):
    rows = value.shape[0]
    half = rows // 2
    after = shifted(value, axis, unit)
    before = shifted(value, axis, -unit)
    far_top = shifted(after[:half], axis, unit)
    far_low = shifted(before[half:], axis, -unit)
    return value, after, (far_top, far_low), before


def joined(block):
    return jnp.concatenate(block, 0) if isinstance(block, tuple) else block


def split3(value):
    high = value.astype(jnp.bfloat16)
    low = (value - high.astype(jnp.float32)).astype(jnp.bfloat16)
    return high, low


def left3(value):
    high, low = split3(value)
    return jnp.concatenate([high, low, high], 1)


def right3(value):
    high, low = split3(value)
    return jnp.concatenate([high, high, low], 0)


def border_kernel(parts, count, places_ref, *refs):
    pieces = refs[:count]
    own_ref, other_ref, out_own, out_other = refs[count : count + 4]
    out_own[...] = jnp.zeros_like(out_own)
    out_other[...] = jnp.zeros_like(out_other)
    for tile, rows in enumerate(parts):
        place = places_ref[tile]

        @pl.when(place >= 0)
        def _():
            at = pl.ds(pl.multiple_of(place * TILE, TILE), TILE)
            right = right3(jnp.concatenate([own_ref[at, :], other_ref[at, :]], 1))
            for index, first in rows:
                left = left3(pieces[index][...])
                product = jnp.dot(left, right, preferred_element_type=jnp.float32)
                span = pl.ds(first, left.shape[0])
                out_own[span, :] += product[:, :TILE]
                out_other[span, :] += product[:, TILE:]


def border_part(blocks, places, own, other):
    arrays = []
    parts = []
    for block in blocks:
        rows = []
        first = 0
        for part in block if isinstance(block, tuple) else (block,):
            rows.append((len(arrays), first))
            arrays.append(part)
            first += part.shape[0]
        parts.append(rows)
    out = jax.ShapeDtypeStruct((blocks[0].shape[0], TILE), jnp.float32)
    vmem = pl.BlockSpec(memory_space=pltpu.VMEM)
    return pl.pallas_call(
        functools.partial(border_kernel, parts, len(arrays)),
        out_shape=(out, out),
        in_specs=[pl.BlockSpec(memory_space=pltpu.SMEM)] + [vmem] * (len(arrays) + 2),
        out_specs=(vmem, vmem),
        compiler_params=pltpu.CompilerParams(vmem_limit_bytes=VMEM_LIMIT),
    )(places, *arrays, own, other)


def inverse_kernel(
    halves, band_tiles, tiles_ref, spots_ref, where_ref, full_ref, *refs
):
    near_ref, far_ref, pivot_ref, border_ref, inverse_ref, chosen = refs
    count = tiles_ref.shape[0]
    me = where_ref[0]
    for q in range(count):
        at = pl.multiple_of(tiles_ref[q] * TILE, TILE)
        high, low = split3(full_ref[pl.ds(at, TILE), :])
        chosen[q, 0] = high
        chosen[q, 1] = low
    for q in range(band_tiles):
        at = pl.multiple_of(tiles_ref[me * band_tiles + q] * TILE, TILE)
        border_ref[pl.ds(q * TILE, TILE), :] = -full_ref[pl.ds(at, TILE), :]
    inverse_ref[...] = pivot_ref[...]
    pieces = near_ref.shape[0]
    for side, held in enumerate((near_ref, far_ref)):
        for piece in range(pieces):
            spot = spots_ref[side * pieces + piece]
            band = spot // halves
            into = pl.ds(pl.multiple_of((spot % halves) * TILE, TILE), TILE)
            total = jnp.zeros((TILE, TILE), jnp.float32)
            for q in range(band_tiles):
                left = left3(held[piece, :, q * TILE : (q + 1) * TILE])
                high = chosen[band * band_tiles + q, 0]
                low = chosen[band * band_tiles + q, 1]
                right = jnp.concatenate([high, high, low], 0)
                total += jnp.dot(left, right, preferred_element_type=jnp.float32)
            inverse_ref[into, :] += total


def inverse_part(full, tiles, spots, here, near, far, pivot, band_tiles):
    count = tiles.shape[0]
    halves = pivot.shape[0] // TILE
    vmem = pl.BlockSpec(memory_space=pltpu.VMEM)
    smem = pl.BlockSpec(memory_space=pltpu.SMEM)
    return pl.pallas_call(
        functools.partial(inverse_kernel, halves, band_tiles),
        out_shape=(
            jax.ShapeDtypeStruct((band_tiles * TILE, TILE), jnp.float32),
            jax.ShapeDtypeStruct(pivot.shape, jnp.float32),
        ),
        in_specs=[smem, smem, smem, vmem, vmem, vmem, vmem],
        out_specs=(vmem, vmem),
        scratch_shapes=[pltpu.VMEM((count, 2, TILE, TILE), jnp.bfloat16)],
        compiler_params=pltpu.CompilerParams(vmem_limit_bytes=VMEM_LIMIT),
    )(tiles, spots, here, full, near, far, pivot)


def gather_rows(value):
    count = lax.axis_size("row")
    copies = jnp.broadcast_to(value[None], (count,) + value.shape)
    got = lax.all_to_all(copies, "row", 0, 0, tiled=True)
    return got.reshape(count * value.shape[0], value.shape[1])


def swap_pairs(fronts):
    groups, rows, cols = (lax.axis_size(a) for a in AXES)
    span = groups // fronts
    slabs = span * cols
    h = slabs // rows
    pairs = []
    for g in range(groups):
        for r in range(rows):
            for c in range(cols):
                s = (g % span) * cols + c
                to_row, to_slab = s // h, r * h + s % h
                to_group = g // span * span + to_slab // cols
                source = (g * rows + r) * cols + c
                target = (to_group * rows + to_row) * cols + to_slab % cols
                pairs.append((source, target))
    return pairs


def places_of(tiles, pool):
    match = tiles[None, :] == jnp.arange(pool, dtype=jnp.int32)[:, None]
    order = jnp.arange(1, tiles.shape[0] + 1, dtype=jnp.int32)
    return jnp.sum(jnp.where(match, order[None, :], 0), axis=1) - 1


def per_device(
    root_inverse, panel_middle, pivot_middle, panel_lower, pivot_lower, tiles_middle, tiles_lower
):
    g = lax.axis_index("grp")
    r = lax.axis_index("row")
    z = lax.axis_index("col")
    x, core = g // 2, g % 2
    xh = x % 2
    steps = jnp.arange(4, dtype=jnp.int32)
    z_order = (z + steps) % 4
    x_order = (x + steps) % 4
    pair_order = jnp.stack([xh, 1 - xh])
    core_order = jnp.stack([core, 1 - core])
    here = r.reshape(1)

    front = lax.dynamic_index_in_dim(tiles_middle, g // 4, 0, keepdims=False)
    root_tiles = (x_order[None, :] * 8 + core * 4 + z_order[:, None]).reshape(-1)
    root_places = places_of(front, 32)[root_tiles]
    middle_spots = (
        (pair_order[None, :, None] * 2 + core_order[:, None, None]) * 4 + z_order[None, None, :]
    ).reshape(-1)
    lower = lax.dynamic_index_in_dim(tiles_lower, x, 0, keepdims=False)
    parent_tiles = (pair_order[None, :] * 8 + core * 4 + z_order[:, None]).reshape(-1)
    parent_places = places_of(lower, 16)[parent_tiles]
    lower_spots = (core_order[:, None] * 4 + z_order[None, :]).reshape(-1)

    with jax.named_scope("root_rows"):
        blocks = []
        for block in ring(root_inverse, "col", 1):
            blocks.extend(ring(joined(block), "grp", 2))
    with jax.named_scope("middle_panel_slab"):
        slab = gather_rows(panel_middle)
        slab_other = crossed(slab, "grp", 1)
    with jax.named_scope("middle_panel_columns"):
        turned = lax.ppermute(panel_middle, AXES, swap_pairs(2)).T
        around = [joined(b) for b in ring(turned, "col", 1)]
        held = jnp.stack(around)
        near = jnp.concatenate([held, crossed(held, "grp", 2)], 0)
        far = crossed(near, "grp", 1)
    with jax.named_scope("lower_panel_slab"):
        lower_slab = gather_rows(panel_lower)
        lower_slab_other = crossed(lower_slab, "grp", 1)
    with jax.named_scope("lower_panel_columns"):
        lower_turned = lax.ppermute(panel_lower, AXES, swap_pairs(4)).T
        lower_near = jnp.stack([joined(b) for b in ring(lower_turned, "col", 1)])
        lower_far = crossed(lower_near, "grp", 1)

    with jax.named_scope("border_middle"):
        mine, theirs = border_part(blocks, root_places, slab, slab_other)
        border = gather_rows(mine + crossed(theirs, "grp", 1))
    with jax.named_scope("inverse_middle"):
        border_middle, inverse_middle = inverse_part(
            border, front, middle_spots, here, near, far, pivot_middle, 3
        )
    with jax.named_scope("parent_rows"):
        blocks = []
        for block in ring(inverse_middle, "col", 1):
            block = joined(block)
            blocks.extend([block, crossed(block, "grp", 2)])
    with jax.named_scope("border_lower"):
        mine, theirs = border_part(blocks, parent_places, lower_slab, lower_slab_other)
        border = gather_rows(mine + crossed(theirs, "grp", 1))
    with jax.named_scope("inverse_lower"):
        border_lower, inverse_lower = inverse_part(
            border, lower, lower_spots, here, lower_near, lower_far, pivot_lower, 1
        )
    return (border_middle, inverse_middle, border_lower, inverse_lower)


def solution(mesh):
    spec = P("row", ("grp", "col"))
    return jax.shard_map(
        per_device,
        mesh=mesh,
        in_specs=(spec, spec, spec, spec, spec, P(), P()),
        out_specs=(spec, spec, spec, spec),
        check_vma=False,
    )
```

```python
import functools

import jax
import jax.numpy as jnp
from jax import lax
from jax.experimental import pallas as pl
from jax.experimental.pallas import tpu as pltpu
from jax.sharding import PartitionSpec as P

TILE = 128
AXES = ("grp", "row", "col")
VMEM_LIMIT = 60 * 1024 * 1024


def shifted(value, axis, step):
    size = lax.axis_size(axis)
    return lax.ppermute(value, axis, [(i, (i - step) % size) for i in range(size)])


def crossed(value, axis, mask):
    size = lax.axis_size(axis)
    return lax.ppermute(value, axis, [(i, i ^ mask) for i in range(size)])


def split3(value):
    high = value.astype(jnp.bfloat16)
    low = (value - high.astype(jnp.float32)).astype(jnp.bfloat16)
    return high, low


def left3(value):
    high, low = split3(value)
    return jnp.concatenate([high, low, high], 1)


def right3(value):
    high, low = split3(value)
    return jnp.concatenate([high, high, low], 0)


def border_kernel(parts, count, places_ref, *refs):
    sources = refs[: count + 2]
    out_own, out_other = refs[count + 2 : count + 4]
    held = refs[count + 4 : -1]
    arrived = refs[-1]
    copies = [
        pltpu.make_async_copy(source, target, arrived.at[i])
        for i, (source, target) in enumerate(zip(sources, held))
    ]
    own_ref, other_ref = held[count:]
    for copy in copies[count:] + copies[:count]:
        copy.start()
    out_own[...] = jnp.zeros_like(out_own)
    out_other[...] = jnp.zeros_like(out_other)
    for copy in copies[count:]:
        copy.wait()
    waited = set()
    for tile, (index, source, size) in enumerate(parts):
        if index not in waited:
            waited.add(index)
            copies[index].wait()
        place = places_ref[tile]

        @pl.when(place >= 0)
        def _():
            at = pl.ds(pl.multiple_of(place, TILE), TILE)
            right = right3(jnp.concatenate([own_ref[at, :], other_ref[at, :]], 1))
            left = left3(held[index][source : source + size, :])
            product = jnp.dot(left, right, preferred_element_type=jnp.float32)
            out_own[...] += product[:, :TILE]
            out_other[...] += product[:, TILE:]


def border_part(arrays, parts, height, places, own, other):
    out = jax.ShapeDtypeStruct((height, TILE), jnp.float32)
    vmem = pl.BlockSpec(memory_space=pltpu.VMEM)
    operands = tuple(arrays) + (own, other)
    return pl.pallas_call(
        functools.partial(border_kernel, parts, len(arrays)),
        out_shape=(out, out),
        in_specs=[pl.BlockSpec(memory_space=pltpu.SMEM)]
        + [pl.BlockSpec(memory_space=pl.ANY)] * len(operands),
        out_specs=(vmem, vmem),
        scratch_shapes=[pltpu.VMEM(one.shape, one.dtype) for one in operands]
        + [pltpu.SemaphoreType.DMA((len(operands),))],
        compiler_params=pltpu.CompilerParams(vmem_limit_bytes=VMEM_LIMIT),
    )(places, *operands)


def inverse_kernel(halves, band_tiles, columns, tiles_ref, spots_ref, where_ref, full_ref, *refs):
    held = refs[:-4]
    pivot_ref, border_ref, inverse_ref, chosen = refs[-4:]
    count = tiles_ref.shape[0]
    me = where_ref[0]
    for q in range(count):
        at = pl.multiple_of(tiles_ref[q] * TILE, TILE)
        high, low = split3(full_ref[pl.ds(at, TILE), :])
        chosen[q, 0] = high
        chosen[q, 1] = low
    for q in range(band_tiles):
        at = pl.multiple_of(tiles_ref[me * band_tiles + q] * TILE, TILE)
        border_ref[pl.ds(q * TILE, TILE), :] = -full_ref[pl.ds(at, TILE), :]
    inverse_ref[...] = pivot_ref[...]
    for piece, (index, slot, column) in enumerate(columns):
        spot = spots_ref[piece]
        band = spot // halves
        into = pl.ds(pl.multiple_of((spot % halves) * TILE, TILE), TILE)
        total = jnp.zeros((TILE, TILE), jnp.float32)
        for q in range(band_tiles):
            left = left3(held[index][slot, :, column + q * TILE : column + (q + 1) * TILE])
            high = chosen[band * band_tiles + q, 0]
            low = chosen[band * band_tiles + q, 1]
            right = jnp.concatenate([high, high, low], 0)
            total += jnp.dot(left, right, preferred_element_type=jnp.float32)
        inverse_ref[into, :] += total


def inverse_part(full, tiles, spots, here, held, columns, pivot, band_tiles):
    count = tiles.shape[0]
    halves = pivot.shape[0] // TILE
    vmem = pl.BlockSpec(memory_space=pltpu.VMEM)
    smem = pl.BlockSpec(memory_space=pltpu.SMEM)
    return pl.pallas_call(
        functools.partial(inverse_kernel, halves, band_tiles, columns),
        out_shape=(
            jax.ShapeDtypeStruct((band_tiles * TILE, TILE), jnp.float32),
            jax.ShapeDtypeStruct(pivot.shape, jnp.float32),
        ),
        in_specs=[smem, smem, smem, vmem] + [vmem] * len(held) + [vmem],
        out_specs=(vmem, vmem),
        scratch_shapes=[pltpu.VMEM((count, 2, TILE, TILE), jnp.bfloat16)],
        compiler_params=pltpu.CompilerParams(vmem_limit_bytes=VMEM_LIMIT),
    )(tiles, spots, here, full, *held, pivot)


def gather_rows(value):
    count = lax.axis_size("row")
    copies = jnp.broadcast_to(value[None], (count,) + value.shape)
    got = lax.all_to_all(copies, "row", 0, 0, tiled=True)
    return got.reshape(-1, value.shape[1])


def swap_pairs(fronts):
    groups, rows, cols = (lax.axis_size(a) for a in AXES)
    span = groups // fronts
    slabs = span * cols
    h = slabs // rows
    pairs = []
    for g in range(groups):
        for r in range(rows):
            for c in range(cols):
                s = (g % span) * cols + c
                to_row, to_slab = s // h, r * h + s % h
                to_group = g // span * span + to_slab // cols
                source = (g * rows + r) * cols + c
                target = (to_group * rows + to_row) * cols + to_slab % cols
                pairs.append((source, target))
    return pairs


def places_of(tiles, pool):
    match = tiles[None, :] == jnp.arange(pool, dtype=jnp.int32)[:, None]
    order = jnp.arange(1, tiles.shape[0] + 1, dtype=jnp.int32)
    return jnp.sum(jnp.where(match, order[None, :], 0), axis=1) - 1


def per_device(
    root_inverse, panel_middle, pivot_middle, panel_lower, pivot_lower, tiles_middle, tiles_lower
):
    g = lax.axis_index("grp")
    r = lax.axis_index("row")
    z = lax.axis_index("col")
    x, core = g // 2, g % 2
    xh = x % 2
    steps = jnp.arange(4, dtype=jnp.int32)
    z_order = (z + steps) % 4
    pair_order = jnp.stack([xh, 1 - xh])
    core_order = jnp.stack([core, 1 - core])
    here = r.reshape(1)

    def row_slot(row):
        return (row // 2 - r // 2) % 4 * 2 + (row + r) % 2

    packed_rows = panel_middle.shape[0] + panel_lower.shape[0]
    front = lax.dynamic_index_in_dim(tiles_middle, g // 4, 0, keepdims=False)
    x_near = jnp.stack([x, (x + 1) % 4, (x + 3) % 4, (x + 2) % 4])
    z_near = jnp.stack([z, (z + 2) % 4, (z + 1) % 4, (z + 3) % 4])
    root_tiles = (core * 4 + x_near[None, :] * 8 + z_near[:, None]).reshape(-1)
    place = places_of(front, 32)[root_tiles]
    root_places = jnp.where(place < 0, -1, row_slot(place // 3) * packed_rows + place % 3 * TILE)
    middle_spots = (
        (pair_order[None, :, None] * 2 + core_order[:, None, None]) * 4 + z_order[None, None, :]
    ).reshape(-1)
    lower = lax.dynamic_index_in_dim(tiles_lower, x, 0, keepdims=False)
    parent_tiles = (pair_order[None, :] * 8 + core * 4 + z_order[:, None]).reshape(-1)
    place = places_of(lower, 16)[parent_tiles]
    parent_places = jnp.where(place < 0, -1, row_slot(place) * packed_rows + panel_middle.shape[0])
    lower_spots = (core_order[:, None] * 4 + z_order[None, :]).reshape(-1)

    own = root_inverse
    full = own.shape[0]
    half = full // 2
    wide = panel_middle.shape[0]
    panel = jnp.concatenate([panel_middle, panel_lower], 0)
    middle = TILE // 2
    tied = lax.optimization_barrier
    with jax.named_scope("step_1"):
        z_after, z_before = shifted(own, "col", 1), shifted(own, "col", -1)
        x_after, x_before = shifted(own, "grp", 2), shifted(own, "grp", -2)
        turned = lax.ppermute(panel_middle, AXES, swap_pairs(2))
        lower_turned = lax.ppermute(panel_lower, AXES, swap_pairs(4))
        panel_other = crossed(panel, "row", 1)
        y_after, y_before = shifted(panel, "row", 2), shifted(panel, "row", -2)
    z_after, z_before, x_after, x_before = tied((z_after, z_before, x_after, x_before))
    with jax.named_scope("step_2"):
        z_top = shifted(z_after[:half], "col", 1)
        z_low = shifted(z_before[half:], "col", -1)
        up_after, up_before = shifted(z_after, "grp", 2), shifted(z_after, "grp", -2)
        down_after, down_before = shifted(z_before, "grp", 2), shifted(z_before, "grp", -2)
        other_after, other_before = shifted(panel_other, "row", 2), shifted(panel_other, "row", -2)
    z_top, z_low, x_after, turned, lower_turned, y_after, y_before = tied(
        (z_top, z_low, x_after, turned, lower_turned, y_after, y_before)
    )
    with jax.named_scope("step_3"):
        far = jnp.concatenate([z_top, z_low], 0)
        far_after, far_before = shifted(far, "grp", 2), shifted(far, "grp", -2)
        x_opposite = shifted(x_after, "grp", 2)
        columns = jnp.concatenate([turned.T, lower_turned.T], 1)
        columns_after, columns_before = shifted(columns, "col", 1), shifted(columns, "col", -1)
        y_opposite = shifted(y_after, "row", 2)
        other_opposite = shifted(other_before, "row", -2)
    (
        up_after, up_before, down_after, down_before, far_after, far_before,
        x_opposite, columns_after, columns_before, y_opposite, other_opposite,
    ) = tied(
        (
            up_after, up_before, down_after, down_before, far_after, far_before,
            x_opposite, columns_after, columns_before, y_opposite, other_opposite,
        )
    )
    with jax.named_scope("step_4"):
        up_opposite = shifted(up_after, "grp", 2)
        down_opposite = shifted(down_before, "grp", -2)
        far_opposite = shifted(far_before, "grp", -2)
        columns_top = shifted(columns_after[:middle], "col", 1)
        columns_low = shifted(columns_before[middle:], "col", -1)
        slab = jnp.concatenate(
            [panel, panel_other, y_after, other_after, y_opposite, other_opposite]
            + [y_before, other_before],
            0,
        )
        slab_other = crossed(slab, "grp", 1)
    slab_other, columns_top, columns_low, up_opposite, down_opposite, far_opposite = tied(
        (slab_other, columns_top, columns_low, up_opposite, down_opposite, far_opposite)
    )
    with jax.named_scope("panel_columns"):
        columns_opposite = jnp.concatenate([columns_top, columns_low], 0)
        columns = jnp.stack([columns, columns_after, columns_opposite, columns_before])
        columns_far = crossed(columns, "grp", 1)
        columns_pair = crossed(columns[:, :, :wide], "grp", 2)
        columns_far_pair = crossed(columns_pair, "grp", 1)
        held = (columns, columns_pair, columns_far, columns_far_pair)
    with jax.named_scope("border_middle"):
        arrays = (own, x_after, x_before, x_opposite)
        arrays += (far, far_after, far_before, far_opposite)
        arrays += (z_after, up_after, up_before, up_opposite)
        arrays += (z_before, down_after, down_before, down_opposite)
        parts = [(k, 0, full) for k in range(len(arrays))]
        mine, theirs = border_part(arrays, parts, full, root_places, slab, slab_other)
        border = gather_rows(mine + crossed(theirs, "grp", 1))
    with jax.named_scope("inverse_middle"):
        spans = [(index, slot, 0) for index in range(4) for slot in range(4)]
        border_middle, inverse_middle = inverse_part(
            border, front, middle_spots, here, held, spans, pivot_middle, 3
        )
    with jax.named_scope("parent_rows"):
        own = inverse_middle
        full = own.shape[0]
        half = full // 2
        z_after, z_before = shifted(own, "col", 1), shifted(own, "col", -1)
        pair = crossed(own, "grp", 2)
        sides = jnp.concatenate([z_after, z_before], 0)
        sides_pair = crossed(sides, "grp", 2)
        z_top = shifted(z_after[:half], "col", 1)
        z_low = shifted(z_before[half:], "col", -1)
        far = jnp.concatenate([z_top, z_low], 0)
        far_pair = crossed(far, "grp", 2)
    with jax.named_scope("border_lower"):
        arrays = (own, pair, z_after, sides_pair, far, far_pair, z_before)
        parts = [(0, 0, full), (1, 0, full), (2, 0, full), (3, 0, full)]
        parts += [(4, 0, full), (5, 0, full), (6, 0, full), (3, full, full)]
        mine, theirs = border_part(arrays, parts, full, parent_places, slab, slab_other)
        border = gather_rows(mine + crossed(theirs, "grp", 1))
    with jax.named_scope("inverse_lower"):
        spans = [(index, slot, wide) for index in range(2) for slot in range(4)]
        border_lower, inverse_lower = inverse_part(
            border, lower, lower_spots, here, (columns, columns_far), spans, pivot_lower, 1
        )
    return (border_middle, inverse_middle, border_lower, inverse_lower)


def solution(mesh):
    spec = P("row", ("grp", "col"))
    return jax.shard_map(
        per_device,
        mesh=mesh,
        in_specs=(spec, spec, spec, spec, spec, P(), P()),
        out_specs=(spec, spec, spec, spec),
        check_vma=False,
    )
```

```python
import functools

import jax
import jax.numpy as jnp
from jax import lax
from jax.experimental import pallas as pl
from jax.experimental.pallas import tpu as pltpu
from jax.sharding import PartitionSpec as P

TILE = 128
AXES = ("grp", "row", "col")
VMEM_LIMIT = 60 * 1024 * 1024


def shifted(value, axis, step):
    size = lax.axis_size(axis)
    return lax.ppermute(value, axis, [(i, (i - step) % size) for i in range(size)])


def crossed(value, axis, mask):
    size = lax.axis_size(axis)
    return lax.ppermute(value, axis, [(i, i ^ mask) for i in range(size)])


def split3(value):
    high = value.astype(jnp.bfloat16)
    low = (value - high.astype(jnp.float32)).astype(jnp.bfloat16)
    return high, low


def left3(value):
    high, low = split3(value)
    return jnp.concatenate([high, low, high], 1)


def right3(value):
    high, low = split3(value)
    return jnp.concatenate([high, high, low], 0)


def border_kernel(parts, count, places_ref, *refs):
    sources = refs[:count]
    panels = refs[count : count + 2]
    out_own, out_other = refs[count + 2 : count + 4]
    held = refs[count + 4 : -3]
    tiles, arrived, ready = refs[-3:]
    copies = [
        pltpu.make_async_copy(source, target, arrived.at[i])
        for i, (source, target) in enumerate(zip(sources, held))
    ]
    fetches = []
    for tile in range(len(parts)):
        at = pl.ds(pl.multiple_of(jnp.maximum(places_ref[tile], 0), TILE), TILE)
        fetches.append(
            [
                pltpu.make_async_copy(panel.at[at, :], tiles.at[tile, side], ready.at[tile, side])
                for side, panel in enumerate(panels)
            ]
        )
    started = set()
    for tile, (index, source, size) in enumerate(parts):
        for fetch in fetches[tile]:
            fetch.start()
        if index not in started:
            started.add(index)
            copies[index].start()
    out_own[...] = jnp.zeros_like(out_own)
    out_other[...] = jnp.zeros_like(out_other)
    waited = set()
    for tile, (index, source, size) in enumerate(parts):
        if index not in waited:
            waited.add(index)
            copies[index].wait()
        for fetch in fetches[tile]:
            fetch.wait()

        @pl.when(places_ref[tile] >= 0)
        def _():
            right = right3(jnp.concatenate([tiles[tile, 0], tiles[tile, 1]], 1))
            left = left3(held[index][source : source + size, :])
            product = jnp.dot(left, right, preferred_element_type=jnp.float32)
            out_own[...] += product[:, :TILE]
            out_other[...] += product[:, TILE:]


def border_part(arrays, parts, height, places, own, other):
    out = jax.ShapeDtypeStruct((height, TILE), jnp.float32)
    vmem = pl.BlockSpec(memory_space=pltpu.VMEM)
    operands = tuple(arrays) + (own, other)
    return pl.pallas_call(
        functools.partial(border_kernel, parts, len(arrays)),
        out_shape=(out, out),
        in_specs=[pl.BlockSpec(memory_space=pltpu.SMEM)]
        + [pl.BlockSpec(memory_space=pl.ANY)] * len(operands),
        out_specs=(vmem, vmem),
        scratch_shapes=[pltpu.VMEM(one.shape, one.dtype) for one in arrays]
        + [
            pltpu.VMEM((len(parts), 2, TILE, TILE), jnp.float32),
            pltpu.SemaphoreType.DMA((len(arrays),)),
            pltpu.SemaphoreType.DMA((len(parts), 2)),
        ],
        compiler_params=pltpu.CompilerParams(vmem_limit_bytes=VMEM_LIMIT),
        cost_estimate=pl.CostEstimate(
            flops=12 * len(parts) * height * TILE * TILE,
            bytes_accessed=32 * len(parts) * height * TILE,
            transcendentals=0,
        ),
    )(places, *operands)


def inverse_kernel(halves, band_tiles, columns, tiles_ref, spots_ref, where_ref, full_ref, *refs):
    held = refs[:-4]
    pivot_ref, border_ref, inverse_ref, chosen = refs[-4:]
    count = tiles_ref.shape[0]
    me = where_ref[0]
    for q in range(count):
        at = pl.multiple_of(tiles_ref[q] * TILE, TILE)
        high, low = split3(full_ref[pl.ds(at, TILE), :])
        chosen[q, 0] = high
        chosen[q, 1] = low
    for q in range(band_tiles):
        at = pl.multiple_of(tiles_ref[me * band_tiles + q] * TILE, TILE)
        border_ref[pl.ds(q * TILE, TILE), :] = -full_ref[pl.ds(at, TILE), :]
    inverse_ref[...] = pivot_ref[...]
    for piece, (index, slot, column) in enumerate(columns):
        spot = spots_ref[piece]
        band = spot // halves
        into = pl.ds(pl.multiple_of((spot % halves) * TILE, TILE), TILE)
        total = jnp.zeros((TILE, TILE), jnp.float32)
        for q in range(band_tiles):
            left = left3(held[index][slot, :, column + q * TILE : column + (q + 1) * TILE])
            high = chosen[band * band_tiles + q, 0]
            low = chosen[band * band_tiles + q, 1]
            right = jnp.concatenate([high, high, low], 0)
            total += jnp.dot(left, right, preferred_element_type=jnp.float32)
        inverse_ref[into, :] += total


def inverse_part(full, tiles, spots, here, held, columns, pivot, band_tiles):
    count = tiles.shape[0]
    halves = pivot.shape[0] // TILE
    vmem = pl.BlockSpec(memory_space=pltpu.VMEM)
    smem = pl.BlockSpec(memory_space=pltpu.SMEM)
    return pl.pallas_call(
        functools.partial(inverse_kernel, halves, band_tiles, columns),
        out_shape=(
            jax.ShapeDtypeStruct((band_tiles * TILE, TILE), jnp.float32),
            jax.ShapeDtypeStruct(pivot.shape, jnp.float32),
        ),
        in_specs=[smem, smem, smem, vmem] + [vmem] * len(held) + [vmem],
        out_specs=(vmem, vmem),
        scratch_shapes=[pltpu.VMEM((count, 2, TILE, TILE), jnp.bfloat16)],
        compiler_params=pltpu.CompilerParams(vmem_limit_bytes=VMEM_LIMIT),
    )(tiles, spots, here, full, *held, pivot)


def gather_rows(value):
    count = lax.axis_size("row")
    copies = jnp.broadcast_to(value[None], (count,) + value.shape)
    got = lax.all_to_all(copies, "row", 0, 0, tiled=True)
    return got.reshape(-1, value.shape[1])


def swap_pairs(fronts):
    groups, rows, cols = (lax.axis_size(a) for a in AXES)
    span = groups // fronts
    slabs = span * cols
    h = slabs // rows
    pairs = []
    for g in range(groups):
        for r in range(rows):
            for c in range(cols):
                s = (g % span) * cols + c
                to_row, to_slab = s // h, r * h + s % h
                to_group = g // span * span + to_slab // cols
                source = (g * rows + r) * cols + c
                target = (to_group * rows + to_row) * cols + to_slab % cols
                pairs.append((source, target))
    return pairs


def places_of(tiles, pool):
    match = tiles[None, :] == jnp.arange(pool, dtype=jnp.int32)[:, None]
    order = jnp.arange(1, tiles.shape[0] + 1, dtype=jnp.int32)
    return jnp.sum(jnp.where(match, order[None, :], 0), axis=1) - 1


def per_device(
    root_inverse, panel_middle, pivot_middle, panel_lower, pivot_lower, tiles_middle, tiles_lower
):
    g = lax.axis_index("grp")
    r = lax.axis_index("row")
    z = lax.axis_index("col")
    x, core = g // 2, g % 2
    xh = x % 2
    steps = jnp.arange(4, dtype=jnp.int32)
    z_order = (z + steps) % 4
    pair_order = jnp.stack([xh, 1 - xh])
    core_order = jnp.stack([core, 1 - core])
    here = r.reshape(1)

    def row_slot(row):
        return row // 2 * 2 + (row + r) % 2

    packed_rows = panel_middle.shape[0] + panel_lower.shape[0]
    front = lax.dynamic_index_in_dim(tiles_middle, g // 4, 0, keepdims=False)
    x_near = jnp.stack([x, (x + 1) % 4, (x + 3) % 4, (x + 2) % 4])
    z_near = jnp.stack([z, (z + 2) % 4, (z + 1) % 4, (z + 3) % 4])
    root_tiles = (core * 4 + x_near[None, :] * 8 + z_near[:, None]).reshape(-1)
    place = places_of(front, 32)[root_tiles]
    root_places = jnp.where(place < 0, -1, row_slot(place // 3) * packed_rows + place % 3 * TILE)
    middle_spots = (
        (pair_order[None, :, None] * 2 + core_order[:, None, None]) * 4 + z_order[None, None, :]
    ).reshape(-1)
    lower = lax.dynamic_index_in_dim(tiles_lower, x, 0, keepdims=False)
    parent_tiles = (pair_order[None, :] * 8 + core * 4 + z_order[:, None]).reshape(-1)
    place = places_of(lower, 16)[parent_tiles]
    parent_places = jnp.where(place < 0, -1, row_slot(place) * packed_rows + panel_middle.shape[0])
    lower_spots = (core_order[:, None] * 4 + z_order[None, :]).reshape(-1)

    same_z = [[0, 2, 4, 6], [1, 3, 5, 7]]
    own = root_inverse
    full = own.shape[0]
    half = full // 2
    wide = panel_middle.shape[0]
    panel = jnp.concatenate([panel_middle, panel_lower], 0)
    middle = TILE // 2
    tied = lax.optimization_barrier
    with jax.named_scope("step_1"):
        z_after, z_before = shifted(own, "col", 1), shifted(own, "col", -1)
        x_after, x_before = shifted(own, "grp", 2), shifted(own, "grp", -2)
        panel_other = crossed(panel, "row", 1)
        panel_pair = jnp.concatenate([panel, panel_other], 0)
        copies = jnp.broadcast_to(panel_pair[None], (4,) + panel_pair.shape)
    z_after, z_before, x_after, x_before, copies = tied(
        (z_after, z_before, x_after, x_before, copies)
    )
    with jax.named_scope("step_2"):
        slab = lax.all_to_all(copies, "row", 0, 0, tiled=True, axis_index_groups=same_z)
        slab = slab.reshape(-1, TILE)
        z_top = shifted(z_after[:half], "col", 1)
        z_low = shifted(z_before[half:], "col", -1)
        up_after, up_before = shifted(z_after, "grp", 2), shifted(z_after, "grp", -2)
        down_after, down_before = shifted(z_before, "grp", 2), shifted(z_before, "grp", -2)
    z_top, z_low, x_after = tied((z_top, z_low, x_after))
    with jax.named_scope("step_3"):
        far = jnp.concatenate([z_top, z_low], 0)
        far_after, far_before = shifted(far, "grp", 2), shifted(far, "grp", -2)
        far_opposite = shifted(far, "grp", 4)
        x_opposite = shifted(x_after, "grp", 2)
        up_after, up_before, down_after, down_before, panel_middle, panel_lower = tied(
            (up_after, up_before, down_after, down_before, panel_middle, panel_lower)
        )
        turned = lax.ppermute(panel_middle, AXES, swap_pairs(2))
        lower_turned = lax.ppermute(panel_lower, AXES, swap_pairs(4))
    (
        up_after, down_before, far_after, far_before, far_opposite, x_opposite,
        slab, turned, lower_turned,
    ) = tied(
        (
            up_after, down_before, far_after, far_before, far_opposite, x_opposite,
            slab, turned, lower_turned,
        )
    )
    with jax.named_scope("step_4"):
        up_opposite = shifted(up_after, "grp", 2)
        down_opposite = shifted(down_before, "grp", -2)
        slab_other = crossed(slab, "grp", 1)
        columns = turned.T
        columns_after, columns_before = shifted(columns, "col", 1), shifted(columns, "col", -1)
    slab_other, columns_after, columns_before, up_opposite, down_opposite = tied(
        (slab_other, columns_after, columns_before, up_opposite, down_opposite)
    )
    with jax.named_scope("panel_columns"):
        middle = TILE // 2
        columns_top = shifted(columns_after[:middle], "col", 1)
        columns_low = shifted(columns_before[middle:], "col", -1)
    with jax.named_scope("border_middle"):
        arrays = (own, x_after, x_before, x_opposite)
        arrays += (far, far_after, far_before, far_opposite)
        arrays += (z_after, up_after, up_before, up_opposite)
        arrays += (z_before, down_after, down_before, down_opposite)
        parts = [(k, 0, full) for k in range(len(arrays))]
        mine, theirs = border_part(arrays, parts, full, root_places, slab, slab_other)
        border = mine + crossed(theirs, "grp", 1)
        border, columns_top, columns_low = tied((border, columns_top, columns_low))
        border = gather_rows(border)
    with jax.named_scope("panel_columns"):
        columns_opposite = jnp.concatenate([columns_top, columns_low], 0)
        columns = jnp.stack([columns, columns_after, columns_opposite, columns_before])
        columns_far = crossed(columns, "grp", 1)
        columns_pair = crossed(columns, "grp", 2)
        held = (columns, columns_pair, columns_far, crossed(columns_pair, "grp", 1))
    with jax.named_scope("inverse_middle"):
        spans = [(index, slot, 0) for index in range(4) for slot in range(4)]
        border_middle, inverse_middle = inverse_part(
            border, front, middle_spots, here, held, spans, pivot_middle, 3
        )
    with jax.named_scope("parent_rows"):
        full = inverse_middle.shape[0]
        lower_turned = lower_turned.T
        packed = jnp.concatenate([lower_turned, inverse_middle], 0)
        z_after, z_before = shifted(packed, "col", 1), shifted(packed, "col", -1)
        pair = crossed(inverse_middle, "grp", 2)
        sides = jnp.concatenate([z_after[TILE:], z_before[TILE:]], 0)
        sides_pair = crossed(sides, "grp", 2)
        z_top = shifted(z_after[: 2 * TILE], "col", 1)
        z_low = shifted(z_before[2 * TILE :], "col", -1)
        far = jnp.concatenate([z_top[TILE:], z_low], 0)
        far_pair = crossed(far, "grp", 2)
    with jax.named_scope("border_lower"):
        arrays = (inverse_middle, pair, sides, sides_pair, far, far_pair)
        parts = [(0, 0, full), (1, 0, full), (2, 0, full), (3, 0, full)]
        parts += [(4, 0, full), (5, 0, full), (2, full, full), (3, full, full)]
        mine, theirs = border_part(arrays, parts, full, parent_places, slab, slab_other)
        border = gather_rows(mine + crossed(theirs, "grp", 1))
    with jax.named_scope("lower_columns"):
        lower_columns = jnp.stack([lower_turned, z_after[:TILE], z_top[:TILE], z_before[:TILE]])
        lower_far = crossed(lower_columns, "grp", 1)
    with jax.named_scope("inverse_lower"):
        spans = [(index, slot, 0) for index in range(2) for slot in range(4)]
        border_lower, inverse_lower = inverse_part(
            border, lower, lower_spots, here, (lower_columns, lower_far), spans, pivot_lower, 1
        )
    return (border_middle, inverse_middle, border_lower, inverse_lower)


def solution(mesh):
    spec = P("row", ("grp", "col"))
    return jax.shard_map(
        per_device,
        mesh=mesh,
        in_specs=(spec, spec, spec, spec, spec, P(), P()),
        out_specs=(spec, spec, spec, spec),
        check_vma=False,
    )
```

```python
import functools

import jax
import jax.numpy as jnp
from jax import lax
from jax.experimental import pallas as pl
from jax.experimental.pallas import tpu as pltpu
from jax.sharding import PartitionSpec as P

TILE = 128
AXES = ("grp", "row", "col")
VMEM_LIMIT = 60 * 1024 * 1024


def shifted(value, axis, step):
    size = lax.axis_size(axis)
    return lax.ppermute(value, axis, [(i, (i - step) % size) for i in range(size)])


def crossed(value, axis, mask):
    size = lax.axis_size(axis)
    return lax.ppermute(value, axis, [(i, i ^ mask) for i in range(size)])


def split3(value):
    high = value.astype(jnp.bfloat16)
    low = (value - high.astype(jnp.float32)).astype(jnp.bfloat16)
    return high, low


def left3(value):
    high, low = split3(value)
    return jnp.concatenate([high, low, high], 1)


def right3(value):
    high, low = split3(value)
    return jnp.concatenate([high, high, low], 0)


def border_kernel(parts, count, places_ref, *refs):
    sources = refs[:count]
    panels = refs[count : count + 2]
    out_own, out_other = refs[count + 2 : count + 4]
    held = refs[count + 4 : -3]
    tiles, arrived, ready = refs[-3:]
    copies = [
        pltpu.make_async_copy(source, target, arrived.at[i])
        for i, (source, target) in enumerate(zip(sources, held))
    ]
    fetches = []
    for tile in range(len(parts)):
        at = pl.ds(pl.multiple_of(jnp.maximum(places_ref[tile], 0), TILE), TILE)
        fetches.append(
            [
                pltpu.make_async_copy(panel.at[at, :], tiles.at[tile, side], ready.at[tile, side])
                for side, panel in enumerate(panels)
            ]
        )
    started = set()
    for tile, (index, source, size) in enumerate(parts):
        for fetch in fetches[tile]:
            fetch.start()
        if index not in started:
            started.add(index)
            copies[index].start()
    out_own[...] = jnp.zeros_like(out_own)
    out_other[...] = jnp.zeros_like(out_other)
    waited = set()
    for tile, (index, source, size) in enumerate(parts):
        if index not in waited:
            waited.add(index)
            copies[index].wait()
        for fetch in fetches[tile]:
            fetch.wait()

        @pl.when(places_ref[tile] >= 0)
        def _():
            right = right3(jnp.concatenate([tiles[tile, 0], tiles[tile, 1]], 1))
            left = left3(held[index][source : source + size, :])
            product = jnp.dot(left, right, preferred_element_type=jnp.float32)
            out_own[...] += product[:, :TILE]
            out_other[...] += product[:, TILE:]


def border_part(arrays, parts, height, places, own, other):
    out = jax.ShapeDtypeStruct((height, TILE), jnp.float32)
    vmem = pl.BlockSpec(memory_space=pltpu.VMEM)
    operands = tuple(arrays) + (own, other)
    return pl.pallas_call(
        functools.partial(border_kernel, parts, len(arrays)),
        out_shape=(out, out),
        in_specs=[pl.BlockSpec(memory_space=pltpu.SMEM)]
        + [pl.BlockSpec(memory_space=pl.ANY)] * len(operands),
        out_specs=(vmem, vmem),
        scratch_shapes=[pltpu.VMEM(one.shape, one.dtype) for one in arrays]
        + [
            pltpu.VMEM((len(parts), 2, TILE, TILE), jnp.float32),
            pltpu.SemaphoreType.DMA((len(arrays),)),
            pltpu.SemaphoreType.DMA((len(parts), 2)),
        ],
        compiler_params=pltpu.CompilerParams(vmem_limit_bytes=VMEM_LIMIT),
        cost_estimate=pl.CostEstimate(
            flops=12 * len(parts) * height * TILE * TILE,
            bytes_accessed=32 * len(parts) * height * TILE,
            transcendentals=0,
        ),
    )(places, *operands)


def inverse_kernel(halves, band_tiles, columns, tiles_ref, spots_ref, where_ref, full_ref, *refs):
    held = refs[:-4]
    pivot_ref, border_ref, inverse_ref, chosen = refs[-4:]
    count = tiles_ref.shape[0]
    me = where_ref[0]
    for q in range(count):
        at = pl.multiple_of(tiles_ref[q] * TILE, TILE)
        high, low = split3(full_ref[pl.ds(at, TILE), :])
        chosen[q, 0] = high
        chosen[q, 1] = low
    for q in range(band_tiles):
        at = pl.multiple_of(tiles_ref[me * band_tiles + q] * TILE, TILE)
        border_ref[pl.ds(q * TILE, TILE), :] = -full_ref[pl.ds(at, TILE), :]
    inverse_ref[...] = pivot_ref[...]
    for piece, (index, slot, column) in enumerate(columns):
        spot = spots_ref[piece]
        band = spot // halves
        into = pl.ds(pl.multiple_of((spot % halves) * TILE, TILE), TILE)
        total = jnp.zeros((TILE, TILE), jnp.float32)
        for q in range(band_tiles):
            left = left3(held[index][slot, :, column + q * TILE : column + (q + 1) * TILE])
            high = chosen[band * band_tiles + q, 0]
            low = chosen[band * band_tiles + q, 1]
            right = jnp.concatenate([high, high, low], 0)
            total += jnp.dot(left, right, preferred_element_type=jnp.float32)
        inverse_ref[into, :] += total


def inverse_part(full, tiles, spots, here, held, columns, pivot, band_tiles):
    count = tiles.shape[0]
    halves = pivot.shape[0] // TILE
    vmem = pl.BlockSpec(memory_space=pltpu.VMEM)
    smem = pl.BlockSpec(memory_space=pltpu.SMEM)
    return pl.pallas_call(
        functools.partial(inverse_kernel, halves, band_tiles, columns),
        out_shape=(
            jax.ShapeDtypeStruct((band_tiles * TILE, TILE), jnp.float32),
            jax.ShapeDtypeStruct(pivot.shape, jnp.float32),
        ),
        in_specs=[smem, smem, smem, vmem] + [vmem] * len(held) + [vmem],
        out_specs=(vmem, vmem),
        scratch_shapes=[pltpu.VMEM((count, 2, TILE, TILE), jnp.bfloat16)],
        compiler_params=pltpu.CompilerParams(vmem_limit_bytes=VMEM_LIMIT),
    )(tiles, spots, here, full, *held, pivot)


def gather_rows(value):
    count = lax.axis_size("row")
    copies = jnp.broadcast_to(value[None], (count,) + value.shape)
    got = lax.all_to_all(copies, "row", 0, 0, tiled=True)
    return got.reshape(-1, value.shape[1])


def swap_pairs(fronts):
    groups, rows, cols = (lax.axis_size(a) for a in AXES)
    span = groups // fronts
    slabs = span * cols
    h = slabs // rows
    pairs = []
    for g in range(groups):
        for r in range(rows):
            for c in range(cols):
                s = (g % span) * cols + c
                to_row, to_slab = s // h, r * h + s % h
                to_group = g // span * span + to_slab // cols
                source = (g * rows + r) * cols + c
                target = (to_group * rows + to_row) * cols + to_slab % cols
                pairs.append((source, target))
    return pairs


def places_of(tiles, pool):
    match = tiles[None, :] == jnp.arange(pool, dtype=jnp.int32)[:, None]
    order = jnp.arange(1, tiles.shape[0] + 1, dtype=jnp.int32)
    return jnp.sum(jnp.where(match, order[None, :], 0), axis=1) - 1


def per_device(
    root_inverse, panel_middle, pivot_middle, panel_lower, pivot_lower, tiles_middle, tiles_lower
):
    g = lax.axis_index("grp")
    r = lax.axis_index("row")
    z = lax.axis_index("col")
    x, core = g // 2, g % 2
    xh = x % 2
    steps = jnp.arange(4, dtype=jnp.int32)
    z_order = (z + steps) % 4
    pair_order = jnp.stack([xh, 1 - xh])
    core_order = jnp.stack([core, 1 - core])
    here = r.reshape(1)

    def row_slot(row):
        return row // 2 * 2 + (row + r) % 2

    packed_rows = panel_middle.shape[0] + panel_lower.shape[0]
    front = lax.dynamic_index_in_dim(tiles_middle, g // 4, 0, keepdims=False)
    x_near = jnp.stack([x, (x + 1) % 4, (x + 3) % 4, (x + 2) % 4])
    z_near = jnp.stack([z, (z + 2) % 4, (z + 1) % 4, (z + 3) % 4])
    root_tiles = (core * 4 + x_near[None, :] * 8 + z_near[:, None]).reshape(-1)
    place = places_of(front, 32)[root_tiles]
    root_places = jnp.where(place < 0, -1, row_slot(place // 3) * packed_rows + place % 3 * TILE)
    middle_spots = (
        (pair_order[None, :, None] * 2 + core_order[:, None, None]) * 4 + z_order[None, None, :]
    ).reshape(-1)
    lower = lax.dynamic_index_in_dim(tiles_lower, x, 0, keepdims=False)
    parent_tiles = (pair_order[None, :] * 8 + core * 4 + z_order[:, None]).reshape(-1)
    place = places_of(lower, 16)[parent_tiles]
    parent_places = jnp.where(place < 0, -1, row_slot(place) * packed_rows + panel_middle.shape[0])
    lower_spots = (core_order[:, None] * 4 + z_order[None, :]).reshape(-1)

    same_z = [[0, 2, 4, 6], [1, 3, 5, 7]]
    own = root_inverse
    full = own.shape[0]
    half = full // 2
    wide = panel_middle.shape[0]
    panel = jnp.concatenate([panel_middle, panel_lower], 0)
    middle = TILE // 2
    tied = lax.optimization_barrier
    with jax.named_scope("step_1"):
        z_after, z_before = shifted(own, "col", 1), shifted(own, "col", -1)
        x_after, x_before = shifted(own, "grp", 2), shifted(own, "grp", -2)
        panel_other = crossed(panel, "row", 1)
        panel_pair = jnp.concatenate([panel, panel_other], 0)
        copies = jnp.broadcast_to(panel_pair[None], (4,) + panel_pair.shape)
    z_after, z_before, x_after, x_before, copies = tied(
        (z_after, z_before, x_after, x_before, copies)
    )
    with jax.named_scope("step_2"):
        slab = lax.all_to_all(copies, "row", 0, 0, tiled=True, axis_index_groups=same_z)
        slab = slab.reshape(-1, TILE)
        z_top = shifted(z_after[:half], "col", 1)
        z_low = shifted(z_before[half:], "col", -1)
        up_after, up_before = shifted(z_after, "grp", 2), shifted(z_after, "grp", -2)
        down_after, down_before = shifted(z_before, "grp", 2), shifted(z_before, "grp", -2)
    z_top, z_low, x_after = tied((z_top, z_low, x_after))
    with jax.named_scope("step_3"):
        far = jnp.concatenate([z_top, z_low], 0)
        far_after, far_before = shifted(far, "grp", 2), shifted(far, "grp", -2)
        far_opposite = shifted(far, "grp", 4)
        x_opposite = shifted(x_after, "grp", 2)
        up_after, up_before, down_after, down_before, panel_middle, panel_lower = tied(
            (up_after, up_before, down_after, down_before, panel_middle, panel_lower)
        )
        turned = lax.ppermute(panel_middle, AXES, swap_pairs(2))
        lower_turned = lax.ppermute(panel_lower, AXES, swap_pairs(4))
    (
        up_after, down_before, far_after, far_before, far_opposite, x_opposite,
        slab, turned, lower_turned,
    ) = tied(
        (
            up_after, down_before, far_after, far_before, far_opposite, x_opposite,
            slab, turned, lower_turned,
        )
    )
    with jax.named_scope("step_4"):
        up_opposite = shifted(up_after, "grp", 2)
        down_opposite = shifted(down_before, "grp", -2)
        slab_other = crossed(slab, "grp", 1)
        columns = turned.T
        columns_after, columns_before = shifted(columns, "col", 1), shifted(columns, "col", -1)
    slab_other, columns_after, columns_before, up_opposite, down_opposite = tied(
        (slab_other, columns_after, columns_before, up_opposite, down_opposite)
    )
    with jax.named_scope("panel_columns"):
        middle = TILE // 2
        columns_top = shifted(columns_after[:middle], "col", 1)
        columns_low = shifted(columns_before[middle:], "col", -1)
    with jax.named_scope("border_middle"):
        arrays = (own, x_after, x_before, x_opposite)
        arrays += (far, far_after, far_before, far_opposite)
        arrays += (z_after, up_after, up_before, up_opposite)
        arrays += (z_before, down_after, down_before, down_opposite)
        parts = [(k, 0, full) for k in range(len(arrays))]
        mine, theirs = border_part(arrays, parts, full, root_places, slab, slab_other)
        border = mine + crossed(theirs, "grp", 1)
        border, columns_top, columns_low = tied((border, columns_top, columns_low))
        border = gather_rows(border)
    with jax.named_scope("panel_columns"):
        columns_opposite = jnp.concatenate([columns_top, columns_low], 0)
        columns = jnp.stack([columns, columns_after, columns_opposite, columns_before])
        columns_far = crossed(columns, "grp", 1)
        columns_pair = crossed(columns, "grp", 2)
        held = (columns, columns_pair, columns_far, crossed(columns_pair, "grp", 1))
    with jax.named_scope("inverse_middle"):
        spans = [(index, slot, 0) for index in range(4) for slot in range(4)]
        border_middle, inverse_middle = inverse_part(
            border, front, middle_spots, here, held, spans, pivot_middle, 3
        )
    with jax.named_scope("parent_rows"):
        full = inverse_middle.shape[0]
        lower_turned = lower_turned.T
        packed = jnp.concatenate([lower_turned, inverse_middle], 0)
        z_after, z_before = shifted(packed, "col", 1), shifted(packed, "col", -1)
        pair = crossed(inverse_middle, "grp", 2)
        sides = jnp.concatenate([z_after[TILE:], z_before[TILE:]], 0)
        sides_pair = crossed(sides, "grp", 2)
        opposite = shifted(z_after, "col", 1)
        far_pair = crossed(opposite[TILE:], "grp", 2)
    with jax.named_scope("border_lower"):
        arrays = (inverse_middle, pair, sides, sides_pair, opposite, far_pair)
        parts = [(0, 0, full), (1, 0, full), (2, 0, full), (3, 0, full)]
        parts += [(4, TILE, full), (5, 0, full), (2, full, full), (3, full, full)]
        mine, theirs = border_part(arrays, parts, full, parent_places, slab, slab_other)
        border = gather_rows(mine + crossed(theirs, "grp", 1))
    with jax.named_scope("lower_columns"):
        lower_columns = jnp.stack([lower_turned, z_after[:TILE], opposite[:TILE], z_before[:TILE]])
        lower_far = crossed(lower_columns, "grp", 1)
    with jax.named_scope("inverse_lower"):
        spans = [(index, slot, 0) for index in range(2) for slot in range(4)]
        border_lower, inverse_lower = inverse_part(
            border, lower, lower_spots, here, (lower_columns, lower_far), spans, pivot_lower, 1
        )
    return (border_middle, inverse_middle, border_lower, inverse_lower)


def solution(mesh):
    spec = P("row", ("grp", "col"))
    return jax.shard_map(
        per_device,
        mesh=mesh,
        in_specs=(spec, spec, spec, spec, spec, P(), P()),
        out_specs=(spec, spec, spec, spec),
        check_vma=False,
    )
```
